32 devices in a mesh: dp: 8 (over z, core), mp: 4 (over y, x).
Axes of the slice: x: 2, y: 2, z: 4, core: 2. Of those that a mesh axis runs over, the one named last changes fastest.
Arguments:
- frames: bfloat16 [1536, 1536], P('dp', 'mp'), may hold values from -6 to 6
- frame_owner: int32 [1536, 1], P('dp'), may hold values from 0 to 7; in each aligned block of 192 rows (0 to 191, 192 to 383, ...) at most 32 rows name the same one
- frame_valid: int32 [1536], P('dp'), may hold values 0 or 1
- norm_gain: float32 [1536], replicated, may hold values from 0.1 to 1.9
- value_weight: bfloat16 [1536, 1536], P('dp', 'mp'), may hold values from -0.15625 to 0.15625
- gate_weight: bfloat16 [1536, 1536], P('dp', 'mp'), may hold values from -0.15625 to 0.15625
- grad_owned: bfloat16 [8, 8, 32, 1536], P('dp', None, None, 'mp'), may hold values from -6 to 6
Outputs:
- gated_owned: bfloat16 [8, 8, 32, 1536], P('dp', None, None, 'mp')
- value_grad: float32 [1536, 1536], P('dp', 'mp')
- gate_grad: float32 [1536, 1536], P('dp', 'mp')
- normed_grad: bfloat16 [8, 8, 32, 1536], P('dp', None, None, 'mp')
The draws below stay inside these ranges and needn't reach their ends.
Inputs may be any that keep to these rules, and one draw needn't show every extreme that they name: `frame_owner`: within the rows of one device (aligned blocks of 192 rows) no owner is named more than 32 times, a bound that some block reaches.
All inputs are finite; a program needn't handle non-finite values. No bound on the sum of `frame_valid` on one device may be relied on, other than what follows from the above.
Results may differ from the reference program's by a relative error of at most 0.013.
Values may be sent and summed in bfloat16 or wider, within the bound.
A program may use at most 64 MiB of HBM per device.

```python
import math
import jax
import jax.numpy as jnp
import numpy as np
from jax import lax

D = 1536
ROWS_DEV = 192
TOKENS = 1536
CAP = 32
N_DP = 8
N_MP = 4


def touch_ends(entries, rng, smallest, high):
    longest = entries.shape.index(max(entries.shape))
    spots = []
    for shift in (0, 1):
        where = [jax.random.randint(jax.random.fold_in(rng, axis), (), 0, length) for axis, length in enumerate(entries.shape)]
        where[longest] = (where[longest] + shift) % entries.shape[longest]
        spots.append(tuple(where))
    return entries.at[spots[0]].set(smallest).at[spots[1]].set(high)


def raised(result, own_key, source, target, shards_of, factor):
    def block_of(position):
        return (jnp.arange(result.shape[position]) // (result.shape[position] // shards_of)).reshape((-1,) + (1,) * (result.ndim - 1 - position))

    one_side = jax.random.permutation(own_key, shards_of)[block_of(target)]
    far = (block_of(target) + shards_of // 2) % shards_of
    return jnp.where((block_of(source) == one_side) | (block_of(source) == far), factor * result, result)


def block_scale(key, dims, cuts, smallest, high):
    def one(dim, parts):
        draws = jax.random.uniform(jax.random.fold_in(jax.random.fold_in(key, 6), dim), (parts,), jnp.float32, smallest / len(cuts), high / len(cuts))
        return jnp.repeat(jnp.exp(draws), dims[dim] // parts).reshape((-1,) + (1,) * (len(dims) - dim - 1))

    gain = one(*cuts[0])
    for cut in cuts[1:]:
        gain = gain * one(*cut)
    return gain


def routed_block(key, own, number, rows, count, top, limit, lean):
    ranking = jax.random.permutation(key, count)
    crowded, usual = portions_of(count, rows * top, limit, lean, True), portions_of(count, rows * top, limit, lean, False)
    places = jnp.arange(count)

    def named(lengths, turn):
        used = int((lengths > 0).sum())
        fixed = max(1, used // 4)
        moved = fixed + (places - fixed + turn * (used - fixed)) % max(1, count - fixed)
        return jnp.zeros((count,), jnp.int32).at[ranking[jnp.where(places < fixed, places, moved)]].set(jnp.asarray(lengths, jnp.int32))

    lengths = jnp.where(number % 4 == 0, named(crowded, number // 4), named(usual, number - number // 4 - 1))
    mixed = jax.random.permutation(jax.random.fold_in(own, 3), count)
    donor, receiver = mixed[0:count // 2 * 2:2], mixed[1:count // 2 * 2:2]
    slack = jnp.minimum(lengths[donor] - 1, limit - lengths[receiver]) // 2
    slack = jnp.where((donor == ranking[0]) | (receiver == ranking[0]) | (lengths[receiver] == 0), 0, jnp.maximum(slack, 0))
    moved = jax.random.randint(jax.random.fold_in(own, 4), (count // 2,), 0, 1 << 20) % (slack + 1)
    lengths = lengths.at[donor].add(-moved).at[receiver].add(moved)
    labels = jnp.searchsorted(jnp.cumsum(lengths), jnp.arange(rows * top), side="right").astype(jnp.int32)
    table = labels.reshape(top, rows).T
    table = table[jax.random.permutation(jax.random.fold_in(own, 1), rows)]
    turn = jax.random.randint(jax.random.fold_in(own, 2), (rows, 1), 0, top)
    return jnp.take_along_axis(table, (jnp.arange(top)[None, :] + turn) % top, axis=1)


def portions_of(number_of, total, limit, lean, full):
    portions = [(1 << 20) // math.isqrt(grade ** lean) + 1 for grade in range(1, number_of + 1)]
    largest = limit if full else min(limit, max(-(-total // number_of), total * portions[0] // sum(portions)))
    least = 1 if total - largest >= number_of - 1 else 0
    given, rest = [largest] + [least] * (number_of - 1), total - largest - least * (number_of - 1)
    while rest > 0:
        free = [i for i in range(1, number_of) if given[i] < largest] or [i for i in range(1, number_of) if given[i] < limit]
        mass, remaining = sum([portions[i] for i in free]), rest
        for i in free:
            more = min(limit - given[i], max(1, remaining * portions[i] // mass), rest)
            given[i] = given[i] + more
            rest = rest - more
    return np.array(given)


def gaussian(rng, extent, width, limit, split=(), held_as=jnp.bfloat16):
    drawn = jax.random.normal(rng, extent, jnp.float32) * width
    if len(split) > 0:
        drawn = block_scale(rng, extent, split, -0.22, 0.18) * drawn
    return jnp.clip(drawn, min=-limit, max=limit).astype(held_as)


def gaussian_with(own_key, shape, deviation, bound, shards, heavy, held_as=jnp.bfloat16):
    drawn = deviation * jax.random.normal(own_key, shape, jnp.float32)
    if shards:
        drawn = drawn * block_scale(own_key, shape, shards, -0.22, 0.18)
    return jnp.clip(raised(drawn, jax.random.fold_in(own_key, 3), *heavy), -bound, bound).astype(held_as)


def setup_inputs(seed: int = 0) -> dict:
    key_list = jax.random.split(jax.random.key(seed), 8)
    frames = gaussian_with(key_list[0], (TOKENS, D), 1.0, 6.0, ((0, 8), (1, 4)), (0, 1, 8, 2.0))
    frame_owner_keys = jax.random.split(jax.random.fold_in(key_list[1], 1), TOKENS // ROWS_DEV)
    frame_owner_turns = jax.random.permutation(jax.random.fold_in(key_list[1], 3), TOKENS // ROWS_DEV)
    frame_owner = jax.vmap(lambda own, number: routed_block(jax.random.fold_in(key_list[1], 2), own, number, ROWS_DEV, N_DP, 1, CAP, 2))(frame_owner_keys, frame_owner_turns).reshape((TOKENS, 1))
    frame_valid = touch_ends((jax.random.randint(key_list[2], (TOKENS,), 0, 8) < 7).astype(jnp.int32), jax.random.fold_in(key_list[2], 1), 0, 1)
    norm_gain = jnp.clip(1.0 + 0.18 * jax.random.normal(key_list[3], (D,), jnp.float32), 0.1, 1.9)
    value_weight = gaussian(key_list[4], (D, D), D ** -0.5, 0.15625, ((0, 8), (1, 4)))
    gate_weight = gaussian(key_list[5], (D, D), D ** -0.5, 0.15625, ((0, 8), (1, 4)))
    grad_owned = gaussian(key_list[6], (N_DP, N_DP, CAP, D), 1.0, 6.0, ((0, 8), (3, 4)))
    return {"frames": frames, "frame_owner": frame_owner, "frame_valid": frame_valid, "norm_gain": norm_gain, "value_weight": value_weight, "gate_weight": gate_weight, "grad_owned": grad_owned}


epsilon = 1e-05

def reference(frames, frame_owner, frame_valid, norm_gain, value_weight, gate_weight, grad_owned):
    owners = frame_owner.reshape(N_DP, ROWS_DEV).astype(jnp.int32)
    positions = jnp.arange(ROWS_DEV, dtype=jnp.int32)
    earlier = positions[None, :] < positions[:, None]
    same_owner = owners[:, :, None] == owners[:, None, :]
    slot_index = lax.optimization_barrier(jnp.sum((same_owner & earlier[None]).astype(jnp.int32), axis=2))
    sources = jnp.arange(N_DP, dtype=jnp.int32)[:, None]
    targets = ((owners * N_DP + sources) * CAP + slot_index).reshape(-1).astype(jnp.int32)
    slot_total = N_DP * N_DP * CAP
    placed = jnp.zeros((slot_total, D), jnp.bfloat16).at[targets].set(frames)
    live_flags = jnp.zeros((slot_total,), jnp.float32).at[targets].set(frame_valid.astype(jnp.float32))
    wide = placed.astype(jnp.float32)
    row_mean = lax.optimization_barrier(jnp.mean(wide, axis=1, keepdims=True))
    centred = wide - row_mean
    row_var = lax.optimization_barrier(jnp.mean(centred * centred, axis=1, keepdims=True))
    normed = (centred * lax.rsqrt(row_var + epsilon) * norm_gain * live_flags[:, None]).astype(jnp.bfloat16)
    value_act = jnp.dot(normed, value_weight, preferred_element_type=jnp.float32)
    gate_act = jnp.dot(normed, gate_weight, preferred_element_type=jnp.float32)
    gate_sig = jax.nn.sigmoid(gate_act)
    gated = (value_act * gate_sig).astype(jnp.bfloat16)
    upstream = grad_owned.reshape(slot_total, D).astype(jnp.float32)
    live_col = live_flags[:, None]
    value_delta = (upstream * gate_sig * live_col).astype(jnp.bfloat16)
    gate_delta = (upstream * value_act * gate_sig * (1.0 - gate_sig) * live_col).astype(jnp.bfloat16)
    scale = float(TOKENS) ** (-0.5)
    value_grad = jnp.dot(normed.T, value_delta, preferred_element_type=jnp.float32) * scale
    gate_grad = jnp.dot(normed.T, gate_delta, preferred_element_type=jnp.float32) * scale
    group_width = D // N_MP
    input_grad = jnp.zeros((slot_total, D), jnp.float32)
    for group in range(N_MP):
        first = group * group_width
        last = first + group_width
        partial_term = jnp.dot(value_delta[:, first:last], value_weight[:, first:last].T, preferred_element_type=jnp.float32) + jnp.dot(gate_delta[:, first:last], gate_weight[:, first:last].T, preferred_element_type=jnp.float32)
        input_grad = input_grad + partial_term.astype(jnp.bfloat16).astype(jnp.float32)
    shape_out = (N_DP, N_DP, CAP, D)
    return (gated.reshape(shape_out), value_grad, gate_grad, input_grad.astype(jnp.bfloat16).reshape(shape_out))
```

```python
import functools
import jax
import jax.numpy as jnp
from jax import lax
from jax.experimental import pallas as pl
from jax.experimental.pallas import tpu as pltpu
from jax.sharding import PartitionSpec as P

epsilon = 1e-05


def normalize_project(whole, slot_live, norm_gain, value_full, gate_full):
    wide = whole.astype(jnp.float32)
    row_mean = jnp.mean(wide, axis=-1, keepdims=True)
    centred = wide - row_mean
    row_var = jnp.mean(centred * centred, axis=-1, keepdims=True)
    normed = (
        centred
        * lax.rsqrt(row_var + epsilon)
        * norm_gain
        * slot_live.astype(jnp.float32)[..., None]
    ).astype(jnp.bfloat16)
    value_act = jnp.einsum("skd,de->ske", normed, value_full, preferred_element_type=jnp.float32)
    gate_act = jnp.einsum("skd,de->ske", normed, gate_full, preferred_element_type=jnp.float32)
    return (normed, value_act, gate_act)


def column_term(normed_flat, delta):
    return lax.dot_general(
        normed_flat, delta, (((0,), (0,)), ((), ())), preferred_element_type=jnp.float32
    )


def plain_body(frames, frame_owner, frame_valid, norm_gain, value_weight, gate_weight, grad_owned):
    peers = lax.axis_size("dp")
    capacity = grad_owned.shape[2]
    row_total = frames.shape[0]
    slot_total = peers * capacity
    dest_owner = frame_owner[:, 0]
    positions = jnp.arange(row_total, dtype=jnp.int32)
    earlier = positions[None, :] < positions[:, None]
    same_owner = dest_owner[:, None] == dest_owner[None, :]
    slot_index = jnp.sum((same_owner & earlier).astype(jnp.int32), axis=1)
    targets = dest_owner * capacity + slot_index
    placing = (jnp.arange(slot_total, dtype=jnp.int32)[:, None] == targets[None, :]).astype(
        jnp.bfloat16
    )
    send_buffer = (
        jnp.dot(placing, frames, preferred_element_type=jnp.float32)
        .astype(jnp.bfloat16)
        .reshape(peers, capacity, -1)
    )
    send_live = (
        jnp.dot(placing, frame_valid.astype(jnp.bfloat16), preferred_element_type=jnp.float32)
        .astype(jnp.bfloat16)
        .reshape(peers, capacity)
    )
    value_full, gate_full = (
        lax.all_gather(value_weight, "dp", axis=0, tiled=True),
        lax.all_gather(gate_weight, "dp", axis=0, tiled=True),
    )
    received_rows, live_recv = (
        lax.all_to_all(send_buffer, "dp", split_axis=0, concat_axis=0, tiled=True),
        lax.all_to_all(send_live, "dp", split_axis=0, concat_axis=0, tiled=True),
    )
    whole = lax.all_gather(received_rows, "mp", axis=2, tiled=True)
    normed, value_act, gate_act = normalize_project(
        whole, live_recv, norm_gain, value_full, gate_full
    )
    normed_flat = normed.reshape(slot_total, -1)
    value_flat = value_act.reshape(slot_total, -1)
    gate_sig = jax.nn.sigmoid(gate_act.reshape(slot_total, -1))
    live_col = live_recv.astype(jnp.float32).reshape(slot_total, 1)
    gated = (value_flat * gate_sig).astype(jnp.bfloat16)
    upstream = grad_owned.reshape(slot_total, -1).astype(jnp.float32)
    value_delta = (upstream * gate_sig * live_col).astype(jnp.bfloat16)
    gate_delta = (upstream * value_flat * gate_sig * (1.0 - gate_sig) * live_col).astype(
        jnp.bfloat16
    )
    scale = float(row_total * peers) ** (-0.5)
    both_delta = jnp.concatenate([value_delta, gate_delta], axis=1)
    both_grad = lax.psum_scatter(
        column_term(normed_flat, both_delta), "dp", scatter_dimension=0, tiled=True
    )
    split_width = value_delta.shape[1]
    value_grad = both_grad[:, :split_width] * scale
    gate_grad = both_grad[:, split_width:] * scale
    contract_last = (((1,), (1,)), ((), ()))
    partial_grad = lax.dot_general(
        value_delta, value_full, contract_last, preferred_element_type=jnp.float32
    ) + lax.dot_general(gate_delta, gate_full, contract_last, preferred_element_type=jnp.float32)
    input_grad = lax.psum_scatter(
        partial_grad.astype(jnp.bfloat16), "mp", scatter_dimension=1, tiled=True
    )
    gated_owned = gated.reshape(1, peers, capacity, -1)
    normed_grad = input_grad.reshape(1, peers, capacity, -1)
    return (gated_owned, value_grad, gate_grad, normed_grad)


filler = 65536.0
MESH = pl.DeviceIdType.MESH


def kernel(
    peers, groups, capacity, scale,
    frames_ref, owner_ref, valid_ref, gain_ref, value_ref, gate_ref, upstream_ref,
    gated_ref, value_grad_ref, gate_grad_ref, input_grad_ref,
    outgoing, whole, weights, normed, normed_t, sibling_t, delta, sibling_delta,
    from_below, from_above, to_above, to_below, term_out, term_in,
    rows_send, rows_recv, mp_send, mp_recv, w_up, w_down, w_side, w_recv,
    t_send, t_recv, d_send, d_recv, up_send, up_recv, down_send, down_recv, x_send, x_recv,
):
    me, column = lax.axis_index("dp"), lax.axis_index("mp")
    chips = peers // 2
    chip, core = me // 2, me % 2
    twin = chip * 2 + 1 - core
    above, below = me + 2, me - 2
    loaded, width = frames_ref.shape
    slots = peers * capacity
    depth = value_ref.shape[0]
    channels = width * groups
    inner, last = chip > 0, chip < chips - 1

    barrier = pltpu.get_barrier_semaphore()
    for step in range(1, peers):
        pl.semaphore_signal(
            barrier, inc=1, device_id={"dp": lax.rem(me + step, peers)}, device_id_type=MESH
        )
    for step in range(1, groups):
        pl.semaphore_signal(
            barrier, inc=1, device_id={"mp": lax.rem(column + step, groups)}, device_id_type=MESH
        )

    owner = owner_ref[...]
    lanes = -(-peers // 128) * 128
    named = (lax.broadcasted_iota(jnp.int32, (loaded, lanes), 1) == owner).astype(jnp.float32)
    first = lax.broadcasted_iota(jnp.int32, (loaded, loaded), 0)
    second = lax.broadcasted_iota(jnp.int32, (loaded, loaded), 1)
    counts = jnp.dot(
        (second < first).astype(jnp.bfloat16), named.astype(jnp.bfloat16),
        preferred_element_type=jnp.float32,
    )
    slot = jnp.sum(named * counts, axis=1, keepdims=True)
    target = owner.astype(jnp.float32) * capacity + slot
    target_row = jnp.sum(jnp.where(first == second, target, 0.0), axis=0, keepdims=True)
    placing = lax.broadcasted_iota(jnp.int32, (slots, loaded), 0) == target_row.astype(jnp.int32)
    present = jnp.sum(
        jnp.where(placing, valid_ref[...].astype(jnp.float32), 0.0), axis=1, keepdims=True
    )
    placed = jnp.dot(
        placing.astype(jnp.bfloat16), frames_ref[...], preferred_element_type=jnp.float32
    )
    outgoing[...] = (
        jnp.where(present > 0.5, placed, filler).astype(jnp.bfloat16).reshape(outgoing.shape)
    )

    pl.semaphore_wait(barrier, peers - 1 + groups - 1)

    def remote(src, dst, send, recv, **device):
        return pltpu.make_async_remote_copy(
            src_ref=src, dst_ref=dst, send_sem=send, recv_sem=recv,
            device_id=device, device_id_type=MESH,
        )

    def rows_copy(step):
        peer = lax.rem(me + step, peers)
        return remote(
            outgoing.at[peer], whole.at[column, me], rows_send.at[peer], rows_recv.at[me], dp=peer
        )

    def rows_arrival(step):
        peer = lax.rem(me + step, peers)
        return remote(
            outgoing.at[peer], whole.at[column, peer], rows_send.at[peer], rows_recv.at[peer], dp=peer
        )

    for step in range(1, peers):
        rows_copy(step).start()
    whole[column, me] = outgoing[me]

    def part(shard, half):
        return weights.at[pl.ds(pl.multiple_of(shard * depth, depth), depth), pl.ds(half * width, width)]

    def weight_copy(where, source, half, peer):
        shard = source * 2 + core
        return remote(
            part(shard, half), part(shard, half), where.at[source, half], w_recv.at[shard, half],
            dp=peer,
        )

    def weight_arrival(shard, half):
        return remote(
            part(shard, half), part(shard, half), w_side.at[0, half], w_recv.at[shard, half], dp=twin
        )

    for half, ref in enumerate((value_ref, gate_ref)):
        weights[pl.ds(pl.multiple_of(me * depth, depth), depth), half * width:(half + 1) * width] = ref[...]
    for half in range(2):
        pl.when(last)(lambda: weight_copy(w_up, chip, half, above).start())
        pl.when(inner)(lambda: weight_copy(w_down, chip, half, below).start())
    for half in range(2):
        weight_copy(w_side, chip, half, twin).start()

    def relay(step):
        for half in range(2):
            @pl.when(chip >= step)
            def _():
                source = chip - step
                weight_arrival(source * 2 + core, half).wait_recv()
                pl.when(last)(lambda: weight_copy(w_up, source, half, above).start())
                weight_copy(w_side, source, half, twin).start()

            @pl.when(chip + step < chips)
            def _():
                source = chip + step
                weight_arrival(source * 2 + core, half).wait_recv()
                pl.when(inner)(lambda: weight_copy(w_down, source, half, below).start())
                weight_copy(w_side, source, half, twin).start()

    for step in range(1, peers):
        rows_arrival(step).wait_recv()

    def mp_copy(step):
        peer = lax.rem(column + step, groups)
        return remote(whole.at[column], whole.at[column], mp_send.at[peer], mp_recv.at[column], mp=peer)

    def mp_arrival(step):
        peer = lax.rem(column + step, groups)
        return remote(whole.at[peer], whole.at[peer], mp_send.at[peer], mp_recv.at[peer], mp=peer)

    for step in range(1, groups):
        mp_copy(step).start()
    early = min(2, chips - 1)
    for step in range(1, early + 1):
        relay(step)
    for step in range(1, groups):
        mp_arrival(step).wait_recv()

    def block(group):
        return whole[group].reshape(slots, width).astype(jnp.float32)

    live = block(0)[:, :1] < 0.5 * filler
    live_col = live.astype(jnp.float32)
    total = jnp.zeros((slots, 1), jnp.float32)
    for group in range(groups):
        total += jnp.sum(block(group), axis=1, keepdims=True)
    row_mean = jnp.where(live, total / channels, 0.0)
    square = jnp.zeros((slots, 1), jnp.float32)
    for group in range(groups):
        centred = jnp.where(live, block(group) - row_mean, 0.0)
        square += jnp.sum(centred * centred, axis=1, keepdims=True)
    factor = lax.rsqrt(square / channels + epsilon)
    for group in range(groups):
        at = slice(group * width, (group + 1) * width)
        centred = jnp.where(live, block(group) - row_mean, 0.0)
        wide = centred * factor * gain_ref[:, at] * live_col
        normed[:, at] = wide.astype(jnp.bfloat16)
        normed_t[at, :] = wide.T.astype(jnp.bfloat16)

    def rows_of(shard):
        return pl.ds(pl.multiple_of(shard * depth, depth), depth)

    def t_copy(target):
        return remote(
            normed_t.at[rows_of(target * 2 + 1 - core)], sibling_t.at[target],
            t_send.at[target], t_recv.at[target], dp=twin,
        )

    for target in range(chips):
        t_copy(target).start()
    for step in range(early + 1, chips):
        relay(step)
    for step in range(chips):
        for half in range(2):
            weight_arrival(step * 2 + 1 - core, half).wait_recv()

    act = jnp.dot(normed[...], weights[...], preferred_element_type=jnp.float32)
    value_act = act[:, :width]
    gate_sig = jax.nn.sigmoid(act[:, width:])
    upstream = upstream_ref[...].astype(jnp.float32)
    gated_ref[...] = (value_act * gate_sig).astype(jnp.bfloat16)
    delta[:, :width] = (upstream * gate_sig * live_col).astype(jnp.bfloat16)
    delta[:, width:] = (upstream * value_act * gate_sig * (1.0 - gate_sig) * live_col).astype(
        jnp.bfloat16
    )
    delta_copy = remote(delta, sibling_delta, d_send.at[0], d_recv.at[0], dp=twin)
    delta_copy.start()

    def term(group):
        rows = weights[pl.ds(pl.multiple_of(group * width, width), width), :]
        return lax.dot_general(
            delta[...], rows, (((1,), (1,)), ((), ())), preferred_element_type=jnp.float32
        ).astype(jnp.bfloat16)

    def x_copy(step):
        peer = lax.rem(column + step, groups)
        return remote(term_out.at[peer], term_in.at[column], x_send.at[peer], x_recv.at[column], mp=peer)

    def x_arrival(step):
        peer = lax.rem(column + step, groups)
        return remote(term_out.at[peer], term_in.at[peer], x_send.at[peer], x_recv.at[peer], mp=peer)

    for step in range(1, groups):
        peer = lax.rem(column + step, groups)
        term_out[peer] = term(peer)
        x_copy(step).start()

    delta_copy.wait_recv()
    for target in range(chips):
        t_copy(target).wait_recv()

    def chip_sum(target):
        return jnp.dot(
            normed_t[rows_of(target * 2 + core), :], delta[...], preferred_element_type=jnp.float32
        ) + jnp.dot(sibling_t[target], sibling_delta[...], preferred_element_type=jnp.float32)

    def up_copy(target):
        return remote(
            to_above.at[target], from_below.at[target], up_send.at[target], up_recv.at[target], dp=above
        )

    def up_arrival(target):
        return remote(
            to_above.at[target], from_below.at[target], up_send.at[target], up_recv.at[target], dp=below
        )

    def down_copy(target):
        return remote(
            to_below.at[target], from_above.at[target], down_send.at[target], down_recv.at[target], dp=below
        )

    def down_arrival(target):
        return remote(
            to_below.at[target], from_above.at[target], down_send.at[target], down_recv.at[target], dp=above
        )

    for step in range(chips - 1, 0, -1):
        @pl.when(chip + step < chips)
        def _():
            target = chip + step
            own = chip_sum(target)

            @pl.when(inner)
            def _():
                up_arrival(target).wait_recv()
                to_above[target] = (own + from_below[target].astype(jnp.float32)).astype(jnp.bfloat16)

            @pl.when(jnp.logical_not(inner))
            def _():
                to_above[target] = own.astype(jnp.bfloat16)

            up_copy(target).start()

        @pl.when(chip >= step)
        def _():
            target = chip - step
            own = chip_sum(target)

            @pl.when(last)
            def _():
                down_arrival(target).wait_recv()
                to_below[target] = (own + from_above[target].astype(jnp.float32)).astype(jnp.bfloat16)

            @pl.when(jnp.logical_not(last))
            def _():
                to_below[target] = own.astype(jnp.bfloat16)

            down_copy(target).start()

    own = chip_sum(chip)
    value_grad_ref[...] = own[:, :width]
    gate_grad_ref[...] = own[:, width:]

    input_grad = term(column).astype(jnp.float32)
    for step in range(1, groups):
        x_arrival(step).wait_recv()
        input_grad += term_in[lax.rem(column + step, groups)].astype(jnp.float32)
    input_grad_ref[...] = input_grad.astype(jnp.bfloat16)

    def add(arrived):
        value_grad_ref[...] += arrived[chip][:, :width].astype(jnp.float32)
        gate_grad_ref[...] += arrived[chip][:, width:].astype(jnp.float32)

    @pl.when(inner)
    def _():
        up_arrival(chip).wait_recv()
        add(from_below)

    @pl.when(last)
    def _():
        down_arrival(chip).wait_recv()
        add(from_above)

    value_grad_ref[...] *= scale
    gate_grad_ref[...] *= scale

    for step in range(1, peers):
        rows_copy(step).wait_send()
    for step in range(1, groups):
        mp_copy(step).wait_send()
        x_copy(step).wait_send()
    delta_copy.wait_send()
    for source in range(chips):
        t_copy(source).wait_send()
        for half in range(2):
            weight_copy(w_side, source, half, twin).wait_send()
            pl.when(last & (source <= chip))(lambda: weight_copy(w_up, source, half, above).wait_send())
            pl.when(inner & (source >= chip))(lambda: weight_copy(w_down, source, half, below).wait_send())
        pl.when(source > chip)(lambda: up_copy(source).wait_send())
        pl.when(source < chip)(lambda: down_copy(source).wait_send())


def body(frames, frame_owner, frame_valid, norm_gain, value_weight, gate_weight, grad_owned):
    peers, groups = lax.axis_size("dp"), lax.axis_size("mp")
    capacity = grad_owned.shape[2]
    loaded, width = frames.shape
    depth = value_weight.shape[0]
    if peers % 2 or depth % 16 or capacity % 16 or loaded % 16 or width % 128 or groups * width != peers * depth:
        return plain_body(
            frames, frame_owner, frame_valid, norm_gain, value_weight, gate_weight, grad_owned
        )
    slots, chips, channels = peers * capacity, peers // 2, width * groups
    half, full = jnp.bfloat16, jnp.float32
    dma = pltpu.SemaphoreType.DMA
    hop = pltpu.VMEM((chips, depth, 2 * width), half)
    vmem = pl.BlockSpec(memory_space=pltpu.VMEM)
    gated, value_grad, gate_grad, input_grad = pl.pallas_call(
        functools.partial(kernel, peers, groups, capacity, float(loaded * peers) ** (-0.5)),
        out_shape=(
            jax.ShapeDtypeStruct((slots, width), half),
            jax.ShapeDtypeStruct((depth, width), full),
            jax.ShapeDtypeStruct((depth, width), full),
            jax.ShapeDtypeStruct((slots, width), half),
        ),
        in_specs=[vmem] * 7,
        out_specs=(vmem,) * 4,
        scratch_shapes=[
            pltpu.VMEM((peers, capacity, width), half),
            pltpu.VMEM((groups, peers, capacity, width), half),
            pltpu.VMEM((channels, 2 * width), half),
            pltpu.VMEM((slots, channels), half),
            pltpu.VMEM((channels, slots), half),
            pltpu.VMEM((chips, depth, slots), half),
            pltpu.VMEM((slots, 2 * width), half),
            pltpu.VMEM((slots, 2 * width), half),
            hop, hop, hop, hop,
            pltpu.VMEM((groups, slots, width), half),
            pltpu.VMEM((groups, slots, width), half),
            dma((peers,)), dma((peers,)), dma((groups,)), dma((groups,)),
            dma((chips, 2)), dma((chips, 2)), dma((chips, 2)), dma((peers, 2)),
            dma((chips,)), dma((chips,)), dma((1,)), dma((1,)),
            dma((chips,)), dma((chips,)), dma((chips,)), dma((chips,)),
            dma((groups,)), dma((groups,)),
        ],
        compiler_params=pltpu.CompilerParams(
            collective_id=0, has_side_effects=True, vmem_limit_bytes=48 * 1024 * 1024
        ),
    )(
        frames, frame_owner, frame_valid.reshape(1, loaded), norm_gain.reshape(1, channels),
        value_weight, gate_weight, grad_owned.reshape(slots, width),
    )
    return (
        gated.reshape(1, peers, capacity, width), value_grad, gate_grad,
        input_grad.reshape(1, peers, capacity, width),
    )


def solution(mesh):
    placed = (
        P("dp", "mp"),
        P("dp", None),
        P("dp"),
        P(),
        P("dp", "mp"),
        P("dp", "mp"),
        P("dp", None, None, "mp"),
    )
    return jax.shard_map(
        body,
        mesh=mesh,
        in_specs=placed,
        out_specs=(
            P("dp", None, None, "mp"),
            P("dp", "mp"),
            P("dp", "mp"),
            P("dp", None, None, "mp"),
        ),
        check_vma=False,
    )
```

```python
import functools
import jax
import jax.numpy as jnp
from jax import lax
from jax.experimental import pallas as pl
from jax.experimental.pallas import tpu as pltpu
from jax.sharding import PartitionSpec as P

epsilon = 1e-05


def normalize_project(whole, slot_live, norm_gain, value_full, gate_full):
    wide = whole.astype(jnp.float32)
    row_mean = jnp.mean(wide, axis=-1, keepdims=True)
    centred = wide - row_mean
    row_var = jnp.mean(centred * centred, axis=-1, keepdims=True)
    normed = (
        centred
        * lax.rsqrt(row_var + epsilon)
        * norm_gain
        * slot_live.astype(jnp.float32)[..., None]
    ).astype(jnp.bfloat16)
    value_act = jnp.einsum("skd,de->ske", normed, value_full, preferred_element_type=jnp.float32)
    gate_act = jnp.einsum("skd,de->ske", normed, gate_full, preferred_element_type=jnp.float32)
    return (normed, value_act, gate_act)


def column_term(normed_flat, delta):
    return lax.dot_general(
        normed_flat, delta, (((0,), (0,)), ((), ())), preferred_element_type=jnp.float32
    )


def plain_body(frames, frame_owner, frame_valid, norm_gain, value_weight, gate_weight, grad_owned):
    peers = lax.axis_size("dp")
    capacity = grad_owned.shape[2]
    row_total = frames.shape[0]
    slot_total = peers * capacity
    dest_owner = frame_owner[:, 0]
    positions = jnp.arange(row_total, dtype=jnp.int32)
    earlier = positions[None, :] < positions[:, None]
    same_owner = dest_owner[:, None] == dest_owner[None, :]
    slot_index = jnp.sum((same_owner & earlier).astype(jnp.int32), axis=1)
    targets = dest_owner * capacity + slot_index
    placing = (jnp.arange(slot_total, dtype=jnp.int32)[:, None] == targets[None, :]).astype(
        jnp.bfloat16
    )
    send_buffer = (
        jnp.dot(placing, frames, preferred_element_type=jnp.float32)
        .astype(jnp.bfloat16)
        .reshape(peers, capacity, -1)
    )
    send_live = (
        jnp.dot(placing, frame_valid.astype(jnp.bfloat16), preferred_element_type=jnp.float32)
        .astype(jnp.bfloat16)
        .reshape(peers, capacity)
    )
    value_full, gate_full = (
        lax.all_gather(value_weight, "dp", axis=0, tiled=True),
        lax.all_gather(gate_weight, "dp", axis=0, tiled=True),
    )
    received_rows, live_recv = (
        lax.all_to_all(send_buffer, "dp", split_axis=0, concat_axis=0, tiled=True),
        lax.all_to_all(send_live, "dp", split_axis=0, concat_axis=0, tiled=True),
    )
    whole = lax.all_gather(received_rows, "mp", axis=2, tiled=True)
    normed, value_act, gate_act = normalize_project(
        whole, live_recv, norm_gain, value_full, gate_full
    )
    normed_flat = normed.reshape(slot_total, -1)
    value_flat = value_act.reshape(slot_total, -1)
    gate_sig = jax.nn.sigmoid(gate_act.reshape(slot_total, -1))
    live_col = live_recv.astype(jnp.float32).reshape(slot_total, 1)
    gated = (value_flat * gate_sig).astype(jnp.bfloat16)
    upstream = grad_owned.reshape(slot_total, -1).astype(jnp.float32)
    value_delta = (upstream * gate_sig * live_col).astype(jnp.bfloat16)
    gate_delta = (upstream * value_flat * gate_sig * (1.0 - gate_sig) * live_col).astype(
        jnp.bfloat16
    )
    scale = float(row_total * peers) ** (-0.5)
    both_delta = jnp.concatenate([value_delta, gate_delta], axis=1)
    both_grad = lax.psum_scatter(
        column_term(normed_flat, both_delta), "dp", scatter_dimension=0, tiled=True
    )
    split_width = value_delta.shape[1]
    value_grad = both_grad[:, :split_width] * scale
    gate_grad = both_grad[:, split_width:] * scale
    contract_last = (((1,), (1,)), ((), ()))
    partial_grad = lax.dot_general(
        value_delta, value_full, contract_last, preferred_element_type=jnp.float32
    ) + lax.dot_general(gate_delta, gate_full, contract_last, preferred_element_type=jnp.float32)
    input_grad = lax.psum_scatter(
        partial_grad.astype(jnp.bfloat16), "mp", scatter_dimension=1, tiled=True
    )
    gated_owned = gated.reshape(1, peers, capacity, -1)
    normed_grad = input_grad.reshape(1, peers, capacity, -1)
    return (gated_owned, value_grad, gate_grad, normed_grad)


filler = 65536.0
MESH = pl.DeviceIdType.MESH


def kernel(
    peers, groups, capacity, scale,
    frames_ref, owner_ref, valid_ref, gain_ref, value_ref, gate_ref, upstream_ref,
    gated_ref, value_grad_ref, gate_grad_ref, input_grad_ref,
    frames_in, owner_in, valid_in, gain_in, upstream_in, outgoing, whole, weights, normed, normed_t, sibling_t, delta, sibling_delta,
    from_below, from_above, to_above, to_below, term_out, term_in,
    in_sem, rows_send, rows_recv, mp_send, mp_recv, w_up, w_down, w_side, w_recv,
    t_send, t_recv, d_send, d_recv, up_send, up_recv, down_send, down_recv, x_send, x_recv,
):
    me, column = lax.axis_index("dp"), lax.axis_index("mp")
    chips = peers // 2
    chip, core = me // 2, me % 2
    twin = chip * 2 + 1 - core
    above, below = me + 2, me - 2
    loaded, width = frames_ref.shape
    cuts = width // 128
    pair = 2 * 128
    slots = peers * capacity
    depth = value_ref.shape[0]
    channels = width * groups
    inner, last = chip > 0, chip < chips - 1

    barrier = pltpu.get_barrier_semaphore()
    for step in range(1, peers):
        pl.semaphore_signal(
            barrier, inc=1, device_id={"dp": lax.rem(me + step, peers)}, device_id_type=MESH
        )
    for step in range(1, groups):
        pl.semaphore_signal(
            barrier, inc=1, device_id={"mp": lax.rem(column + step, groups)}, device_id_type=MESH
        )

    loads = []
    for ref, held in (
        (owner_ref, owner_in), (valid_ref, valid_in), (frames_ref, frames_in), (gain_ref, gain_in),
        (upstream_ref, upstream_in),
    ):
        loads.append(pltpu.make_async_copy(ref, held, in_sem.at[len(loads)]))
    own_rows = pl.ds(pl.multiple_of(me * depth, depth), depth)
    for cut in range(cuts):
        for side, ref in enumerate((value_ref, gate_ref)):
            loads.append(
                pltpu.make_async_copy(
                    ref.at[:, pl.ds(cut * 128, 128)],
                    weights.at[cut, own_rows, pl.ds(side * 128, 128)],
                    in_sem.at[len(loads)],
                )
            )
    for load in loads:
        load.start()
    for load in loads[:3]:
        load.wait()

    first = lax.broadcasted_iota(jnp.int32, (loaded, loaded), 0)
    second = lax.broadcasted_iota(jnp.int32, (loaded, loaded), 1)
    owner = jnp.sum(
        jnp.where(first == second, owner_in[...].astype(jnp.float32), 0.0), axis=1, keepdims=True
    )
    lanes = -(-peers // 128) * 128
    named = (lax.broadcasted_iota(jnp.int32, (loaded, lanes), 1) == owner.astype(jnp.int32)).astype(
        jnp.float32
    )
    counts = jnp.dot(
        (second < first).astype(jnp.bfloat16), named.astype(jnp.bfloat16),
        preferred_element_type=jnp.float32,
    )
    slot = jnp.sum(named * counts, axis=1, keepdims=True)
    target = owner * capacity + slot
    target_row = jnp.sum(jnp.where(first == second, target, 0.0), axis=0, keepdims=True)
    placing = lax.broadcasted_iota(jnp.int32, (slots, loaded), 0) == target_row.astype(jnp.int32)
    present = jnp.sum(
        jnp.where(placing, valid_in[...].astype(jnp.float32), 0.0), axis=1, keepdims=True
    )
    placed = jnp.dot(
        placing.astype(jnp.bfloat16), frames_in[...], preferred_element_type=jnp.float32
    )
    outgoing[...] = (
        jnp.where(present > 0.5, placed, filler).astype(jnp.bfloat16).reshape(outgoing.shape)
    )

    pl.semaphore_wait(barrier, peers - 1 + groups - 1)

    def remote(src, dst, send, recv, **device):
        return pltpu.make_async_remote_copy(
            src_ref=src, dst_ref=dst, send_sem=send, recv_sem=recv,
            device_id=device, device_id_type=MESH,
        )

    def rows_copy(step):
        peer = lax.rem(me + step, peers)
        return remote(
            outgoing.at[peer], whole.at[column, me], rows_send.at[peer], rows_recv.at[me], dp=peer
        )

    def rows_arrival(step):
        peer = lax.rem(me + peers - step, peers)
        return remote(
            outgoing.at[peer], whole.at[column, peer], rows_send.at[peer], rows_recv.at[peer], dp=peer
        )

    for step in range(1, peers):
        rows_copy(step).start()
    whole[column, me] = outgoing[me]

    def part(shard, cut):
        return weights.at[cut, pl.ds(pl.multiple_of(shard * depth, depth), depth)]

    def weight_copy(where, source, cut, peer):
        shard = source * 2 + core
        return remote(
            part(shard, cut), part(shard, cut), where.at[source, cut], w_recv.at[shard, cut], dp=peer
        )

    def weight_arrival(shard, cut):
        return remote(
            part(shard, cut), part(shard, cut), w_side.at[0, cut], w_recv.at[shard, cut], dp=twin
        )

    for cut in range(cuts):
        for load in loads[5 + 2 * cut:7 + 2 * cut]:
            load.wait()
        pl.when(last)(lambda: weight_copy(w_up, chip, cut, above).start())
        pl.when(inner)(lambda: weight_copy(w_down, chip, cut, below).start())
        weight_copy(w_side, chip, cut, twin).start()

    def relay(cut, step, onward):
        @pl.when((chip >= step) & (last if onward else jnp.logical_not(last)))
        def _():
            source = chip - step
            weight_arrival(source * 2 + core, cut).wait_recv()
            if onward:
                weight_copy(w_up, source, cut, above).start()
            weight_copy(w_side, source, cut, twin).start()

        @pl.when((chip + step < chips) & (inner if onward else jnp.logical_not(inner)))
        def _():
            source = chip + step
            weight_arrival(source * 2 + core, cut).wait_recv()
            if onward:
                weight_copy(w_down, source, cut, below).start()
            weight_copy(w_side, source, cut, twin).start()

    def mp_copy(step, owned):
        peer = lax.rem(column + step, groups)
        return remote(
            whole.at[column, owned], whole.at[column, owned], mp_send.at[peer, owned],
            mp_recv.at[column, owned], mp=peer,
        )

    def mp_arrival(step, owned):
        peer = lax.rem(column + step, groups)
        return remote(
            whole.at[peer, owned], whole.at[peer, owned], mp_send.at[peer, owned],
            mp_recv.at[peer, owned], mp=peer,
        )

    for behind in range(peers):
        if behind:
            rows_arrival(behind).wait_recv()
        for step in range(1, groups):
            mp_copy(step, lax.rem(me + peers - behind, peers)).start()
    for step in range(1, chips):
        relay(0, step, True)
    ahead = [(cut, step) for cut in range(1, cuts) for step in range(1, chips)]
    for cut, step in ahead[:1]:
        relay(cut, step, True)
    for behind in range(peers):
        for step in range(1, groups):
            mp_arrival(step, lax.rem(me + peers - behind, peers)).wait_recv()
    loads[3].wait()
    loads[4].wait()
    gain = gain_in[...].reshape(1, channels)

    def block(group):
        return whole[group].reshape(slots, width).astype(jnp.float32)

    live = block(0)[:, :1] < 0.5 * filler
    live_col = live.astype(jnp.float32)
    total = jnp.zeros((slots, 1), jnp.float32)
    for group in range(groups):
        total += jnp.sum(block(group), axis=1, keepdims=True)
    row_mean = jnp.where(live, total / channels, 0.0)
    square = jnp.zeros((slots, 1), jnp.float32)
    for group in range(groups):
        centred = jnp.where(live, block(group) - row_mean, 0.0)
        square += jnp.sum(centred * centred, axis=1, keepdims=True)
    factor = lax.rsqrt(square / channels + epsilon)
    for group in range(groups):
        at = slice(group * width, (group + 1) * width)
        centred = jnp.where(live, block(group) - row_mean, 0.0)
        wide = centred * factor * gain[:, at] * live_col
        normed[:, at] = wide.astype(jnp.bfloat16)
        normed_t[at, :] = wide.T.astype(jnp.bfloat16)

    def rows_of(shard):
        return pl.ds(pl.multiple_of(shard * depth, depth), depth)

    def t_copy(target):
        return remote(
            normed_t.at[rows_of(target * 2 + 1 - core)], sibling_t.at[target],
            t_send.at[target], t_recv.at[target], dp=twin,
        )

    for target in range(chips):
        t_copy(target).start()
    def delta_copy(cut):
        return remote(delta.at[cut], sibling_delta.at[cut], d_send.at[cut], d_recv.at[cut], dp=twin)

    def project(cut):
        for step in range(1, chips):
            relay(cut, step, False)
        for source in range(chips):
            weight_arrival(source * 2 + 1 - core, cut).wait_recv()
        act = jnp.dot(normed[...], weights[cut], preferred_element_type=jnp.float32)
        at = slice(cut * 128, (cut + 1) * 128)
        value_act = act[:, :128]
        gate_sig = jax.nn.sigmoid(act[:, 128:])
        upstream = upstream_in[:, at].astype(jnp.float32)
        delta[cut, :, :128] = (upstream * gate_sig * live_col).astype(jnp.bfloat16)
        delta[cut, :, 128:] = (
            upstream * value_act * gate_sig * (1.0 - gate_sig) * live_col
        ).astype(jnp.bfloat16)
        delta_copy(cut).start()
        gated_ref[:, at] = (value_act * gate_sig).astype(jnp.bfloat16)

    def term(group):
        rows = pl.ds(pl.multiple_of(group * width, width), width)
        result = jnp.zeros((slots, width), jnp.float32)
        for cut in range(cuts):
            result += lax.dot_general(
                delta[cut], weights[cut, rows, :], (((1,), (1,)), ((), ())),
                preferred_element_type=jnp.float32,
            )
        return result.astype(jnp.bfloat16)

    def x_copy(step):
        peer = lax.rem(column + step, groups)
        return remote(term_out.at[peer], term_in.at[column], x_send.at[peer], x_recv.at[column], mp=peer)

    def x_arrival(step):
        peer = lax.rem(column + step, groups)
        return remote(term_out.at[peer], term_in.at[peer], x_send.at[peer], x_recv.at[peer], mp=peer)

    def chip_sum(target, cut):
        return jnp.dot(
            normed_t[rows_of(target * 2 + core), :], delta[cut], preferred_element_type=jnp.float32
        ) + jnp.dot(sibling_t[target], sibling_delta[cut], preferred_element_type=jnp.float32)

    def hop(out, into, send, recv, target, cut, peer):
        return remote(
            out.at[cut, target], into.at[cut, target], send.at[cut, target], recv.at[cut, target],
            dp=peer,
        )

    def up(target, cut, peer):
        return hop(to_above, from_below, up_send, up_recv, target, cut, peer)

    def down(target, cut, peer):
        return hop(to_below, from_above, down_send, down_recv, target, cut, peer)

    def send_sum(copy, out, into, target, cut, onward, behind, ahead):
        own = chip_sum(target, cut)

        @pl.when(onward)
        def _():
            copy(target, cut, behind).wait_recv()
            out[cut, target] = (own + into[cut, target].astype(jnp.float32)).astype(jnp.bfloat16)

        @pl.when(jnp.logical_not(onward))
        def _():
            out[cut, target] = own.astype(jnp.bfloat16)

        copy(target, cut, ahead).start()

    def chain(cut):
        for step in range(chips - 1, 0, -1):
            @pl.when(chip + step < chips)
            def _():
                send_sum(up, to_above, from_below, chip + step, cut, inner, below, above)

            @pl.when(chip >= step)
            def _():
                send_sum(down, to_below, from_above, chip - step, cut, last, above, below)

    project(0)
    for cut, step in ahead[1:]:
        relay(cut, step, True)
    for target in range(chips):
        t_copy(target).wait_recv()
    for cut in range(cuts):
        delta_copy(cut).wait_recv()
        if cut == cuts - 1:
            for step in range(1, groups):
                peer = lax.rem(column + step, groups)
                term_out[peer] = term(peer)
                x_copy(step).start()
        chain(cut)
        if cut < cuts - 1:
            project(cut + 1)

    for cut in range(cuts):
        at = slice(cut * 128, (cut + 1) * 128)
        own = chip_sum(chip, cut)
        value_grad_ref[:, at] = own[:, :128]
        gate_grad_ref[:, at] = own[:, 128:]

    input_grad = term(column).astype(jnp.float32)
    for step in range(1, groups):
        x_arrival(step).wait_recv()
        input_grad += term_in[lax.rem(column + step, groups)].astype(jnp.float32)
    input_grad_ref[...] = input_grad.astype(jnp.bfloat16)

    def add(arrived, cut):
        at = slice(cut * 128, (cut + 1) * 128)
        value_grad_ref[:, at] += arrived[cut, chip, :, :128].astype(jnp.float32)
        gate_grad_ref[:, at] += arrived[cut, chip, :, 128:].astype(jnp.float32)

    for cut in range(cuts):
        @pl.when(inner)
        def _():
            up(chip, cut, below).wait_recv()
            add(from_below, cut)

        @pl.when(last)
        def _():
            down(chip, cut, above).wait_recv()
            add(from_above, cut)

    value_grad_ref[...] *= scale
    gate_grad_ref[...] *= scale

    for step in range(1, peers):
        rows_copy(step).wait_send()
    for step in range(1, groups):
        for owned in range(peers):
            mp_copy(step, owned).wait_send()
        x_copy(step).wait_send()
    for source in range(chips):
        t_copy(source).wait_send()
    for cut in range(cuts):
        delta_copy(cut).wait_send()
        for source in range(chips):
            weight_copy(w_side, source, cut, twin).wait_send()
            pl.when(last & (source <= chip))(lambda: weight_copy(w_up, source, cut, above).wait_send())
            pl.when(inner & (source >= chip))(lambda: weight_copy(w_down, source, cut, below).wait_send())
            pl.when(source > chip)(lambda: up(source, cut, above).wait_send())
            pl.when(source < chip)(lambda: down(source, cut, below).wait_send())


def write_out(*refs):
    count = len(refs) // 2
    copies = [pltpu.make_async_copy(refs[i], refs[count + i], refs[-1].at[i]) for i in range(count)]
    for copy in copies:
        copy.start()
    for copy in copies:
        copy.wait()


def body(frames, frame_owner, frame_valid, norm_gain, value_weight, gate_weight, grad_owned):
    peers, groups = lax.axis_size("dp"), lax.axis_size("mp")
    capacity = grad_owned.shape[2]
    loaded, width = frames.shape
    depth = value_weight.shape[0]
    if peers % 2 or depth % 16 or capacity % 16 or loaded % 16 or width % 128 or groups * width != peers * depth:
        return plain_body(
            frames, frame_owner, frame_valid, norm_gain, value_weight, gate_weight, grad_owned
        )
    slots, chips, channels = peers * capacity, peers // 2, width * groups
    cuts = width // 128
    half, full = jnp.bfloat16, jnp.float32
    dma = pltpu.SemaphoreType.DMA
    hop = pltpu.VMEM((cuts, chips, depth, 256), half)
    deltas = pltpu.VMEM((cuts, slots, 256), half)
    vmem, hbm = pl.BlockSpec(memory_space=pltpu.VMEM), pl.BlockSpec(memory_space=pltpu.HBM)
    outs = (
        jax.ShapeDtypeStruct((slots, width), half),
        jax.ShapeDtypeStruct((depth, width), full),
        jax.ShapeDtypeStruct((depth, width), full),
        jax.ShapeDtypeStruct((slots, width), half),
    )
    results = pl.pallas_call(
        functools.partial(kernel, peers, groups, capacity, float(loaded * peers) ** (-0.5)),
        out_shape=outs,
        in_specs=[hbm] * 7,
        out_specs=(vmem,) * 4,
        scratch_shapes=[
            pltpu.VMEM((loaded, width), half),
            pltpu.VMEM((1, loaded), jnp.int32),
            pltpu.VMEM((1, loaded), jnp.int32),
            pltpu.VMEM((channels,), full),
            pltpu.VMEM((slots, width), half),
            pltpu.VMEM((peers, capacity, width), half),
            pltpu.VMEM((groups, peers, capacity, width), half),
            pltpu.VMEM((cuts, channels, 256), half),
            pltpu.VMEM((slots, channels), half),
            pltpu.VMEM((channels, slots), half),
            pltpu.VMEM((chips, depth, slots), half),
            deltas, deltas,
            hop, hop, hop, hop,
            pltpu.VMEM((groups, slots, width), half),
            pltpu.VMEM((groups, slots, width), half),
            dma((5 + 2 * cuts,)),
            dma((peers,)), dma((peers,)), dma((groups, peers)), dma((groups, peers)),
            dma((chips, cuts)), dma((chips, cuts)), dma((chips, cuts)), dma((peers, cuts)),
            dma((chips,)), dma((chips,)), dma((cuts,)), dma((cuts,)),
            dma((cuts, chips)), dma((cuts, chips)), dma((cuts, chips)), dma((cuts, chips)),
            dma((groups,)), dma((groups,)),
        ],
        compiler_params=pltpu.CompilerParams(
            collective_id=0, has_side_effects=True, vmem_limit_bytes=63 * 1024 * 1024
        ),
    )(
        frames, frame_owner.reshape(1, loaded), frame_valid.reshape(1, loaded), norm_gain,
        value_weight, gate_weight, grad_owned.reshape(slots, width),
    )
    gated, value_grad, gate_grad, input_grad = pl.pallas_call(
        write_out,
        out_shape=outs,
        in_specs=[hbm] * 4,
        out_specs=(hbm,) * 4,
        scratch_shapes=[dma((4,))],
    )(*results)
    return (
        gated.reshape(1, peers, capacity, width), value_grad, gate_grad,
        input_grad.reshape(1, peers, capacity, width),
    )


def solution(mesh):
    placed = (
        P("dp", "mp"),
        P("dp", None),
        P("dp"),
        P(),
        P("dp", "mp"),
        P("dp", "mp"),
        P("dp", None, None, "mp"),
    )
    return jax.shard_map(
        body,
        mesh=mesh,
        in_specs=placed,
        out_specs=(
            P("dp", None, None, "mp"),
            P("dp", "mp"),
            P("dp", "mp"),
            P("dp", None, None, "mp"),
        ),
        check_vma=False,
    )
```

```python
import functools
import jax
import jax.numpy as jnp
from jax import lax
from jax.experimental import pallas as pl
from jax.experimental.pallas import tpu as pltpu
from jax.sharding import PartitionSpec as P

epsilon = 1e-05


def normalize_project(whole, slot_live, norm_gain, value_full, gate_full):
    wide = whole.astype(jnp.float32)
    row_mean = jnp.mean(wide, axis=-1, keepdims=True)
    centred = wide - row_mean
    row_var = jnp.mean(centred * centred, axis=-1, keepdims=True)
    normed = (
        centred
        * lax.rsqrt(row_var + epsilon)
        * norm_gain
        * slot_live.astype(jnp.float32)[..., None]
    ).astype(jnp.bfloat16)
    value_act = jnp.einsum("skd,de->ske", normed, value_full, preferred_element_type=jnp.float32)
    gate_act = jnp.einsum("skd,de->ske", normed, gate_full, preferred_element_type=jnp.float32)
    return (normed, value_act, gate_act)


def column_term(normed_flat, delta):
    return lax.dot_general(
        normed_flat, delta, (((0,), (0,)), ((), ())), preferred_element_type=jnp.float32
    )


def plain_body(frames, frame_owner, frame_valid, norm_gain, value_weight, gate_weight, grad_owned):
    peers = lax.axis_size("dp")
    capacity = grad_owned.shape[2]
    row_total = frames.shape[0]
    slot_total = peers * capacity
    dest_owner = frame_owner[:, 0]
    positions = jnp.arange(row_total, dtype=jnp.int32)
    earlier = positions[None, :] < positions[:, None]
    same_owner = dest_owner[:, None] == dest_owner[None, :]
    slot_index = jnp.sum((same_owner & earlier).astype(jnp.int32), axis=1)
    targets = dest_owner * capacity + slot_index
    placing = (jnp.arange(slot_total, dtype=jnp.int32)[:, None] == targets[None, :]).astype(
        jnp.bfloat16
    )
    send_buffer = (
        jnp.dot(placing, frames, preferred_element_type=jnp.float32)
        .astype(jnp.bfloat16)
        .reshape(peers, capacity, -1)
    )
    send_live = (
        jnp.dot(placing, frame_valid.astype(jnp.bfloat16), preferred_element_type=jnp.float32)
        .astype(jnp.bfloat16)
        .reshape(peers, capacity)
    )
    value_full, gate_full = (
        lax.all_gather(value_weight, "dp", axis=0, tiled=True),
        lax.all_gather(gate_weight, "dp", axis=0, tiled=True),
    )
    received_rows, live_recv = (
        lax.all_to_all(send_buffer, "dp", split_axis=0, concat_axis=0, tiled=True),
        lax.all_to_all(send_live, "dp", split_axis=0, concat_axis=0, tiled=True),
    )
    whole = lax.all_gather(received_rows, "mp", axis=2, tiled=True)
    normed, value_act, gate_act = normalize_project(
        whole, live_recv, norm_gain, value_full, gate_full
    )
    normed_flat = normed.reshape(slot_total, -1)
    value_flat = value_act.reshape(slot_total, -1)
    gate_sig = jax.nn.sigmoid(gate_act.reshape(slot_total, -1))
    live_col = live_recv.astype(jnp.float32).reshape(slot_total, 1)
    gated = (value_flat * gate_sig).astype(jnp.bfloat16)
    upstream = grad_owned.reshape(slot_total, -1).astype(jnp.float32)
    value_delta = (upstream * gate_sig * live_col).astype(jnp.bfloat16)
    gate_delta = (upstream * value_flat * gate_sig * (1.0 - gate_sig) * live_col).astype(
        jnp.bfloat16
    )
    scale = float(row_total * peers) ** (-0.5)
    both_delta = jnp.concatenate([value_delta, gate_delta], axis=1)
    both_grad = lax.psum_scatter(
        column_term(normed_flat, both_delta), "dp", scatter_dimension=0, tiled=True
    )
    split_width = value_delta.shape[1]
    value_grad = both_grad[:, :split_width] * scale
    gate_grad = both_grad[:, split_width:] * scale
    contract_last = (((1,), (1,)), ((), ()))
    partial_grad = lax.dot_general(
        value_delta, value_full, contract_last, preferred_element_type=jnp.float32
    ) + lax.dot_general(gate_delta, gate_full, contract_last, preferred_element_type=jnp.float32)
    input_grad = lax.psum_scatter(
        partial_grad.astype(jnp.bfloat16), "mp", scatter_dimension=1, tiled=True
    )
    gated_owned = gated.reshape(1, peers, capacity, -1)
    normed_grad = input_grad.reshape(1, peers, capacity, -1)
    return (gated_owned, value_grad, gate_grad, normed_grad)


filler = 65536.0
MESH = pl.DeviceIdType.MESH


def kernel(
    peers, groups, capacity, scale,
    frames_ref, owner_ref, valid_ref, gain_ref, value_ref, gate_ref, upstream_ref,
    gated_ref, value_grad_ref, gate_grad_ref, input_grad_ref,
    frames_in, owner_in, valid_in, gain_in, upstream_in, outgoing, whole, weights, normed, normed_t, sibling_t, delta, sibling_delta,
    from_below, from_above, to_above, to_below, term_out, term_in,
    in_sem, rows_send, rows_recv, mp_send, mp_recv, w_up, w_down, w_side, w_recv,
    t_send, t_recv, d_send, d_recv, up_send, up_recv, down_send, down_recv, x_send, x_recv,
):
    me, column = lax.axis_index("dp"), lax.axis_index("mp")
    chips = peers // 2
    chip, core = me // 2, me % 2
    twin = chip * 2 + 1 - core
    above, below = me + 2, me - 2
    loaded, width = frames_ref.shape
    cuts = width // 128
    pair = 2 * 128
    slots = peers * capacity
    depth = value_ref.shape[0]
    channels = width * groups
    inner, last = chip > 0, chip < chips - 1

    barrier = pltpu.get_barrier_semaphore()
    for step in range(1, peers):
        pl.semaphore_signal(
            barrier, inc=1, device_id={"dp": lax.rem(me + step, peers)}, device_id_type=MESH
        )
    for step in range(1, groups):
        pl.semaphore_signal(
            barrier, inc=1, device_id={"mp": lax.rem(column + step, groups)}, device_id_type=MESH
        )

    loads = []
    for ref, held in (
        (owner_ref, owner_in), (valid_ref, valid_in), (frames_ref, frames_in), (gain_ref, gain_in),
        (upstream_ref, upstream_in),
    ):
        loads.append(pltpu.make_async_copy(ref, held, in_sem.at[len(loads)]))
    own_rows = pl.ds(pl.multiple_of(me * depth, depth), depth)
    for cut in range(cuts):
        for side, ref in enumerate((value_ref, gate_ref)):
            loads.append(
                pltpu.make_async_copy(
                    ref.at[:, pl.ds(cut * 128, 128)],
                    weights.at[cut, own_rows, pl.ds(side * 128, 128)],
                    in_sem.at[len(loads)],
                )
            )
    for load in loads:
        load.start()
    for load in loads[:3]:
        load.wait()

    first = lax.broadcasted_iota(jnp.int32, (loaded, loaded), 0)
    second = lax.broadcasted_iota(jnp.int32, (loaded, loaded), 1)
    owner = jnp.sum(
        jnp.where(first == second, owner_in[...].astype(jnp.float32), 0.0), axis=1, keepdims=True
    )
    lanes = -(-peers // 128) * 128
    named = (lax.broadcasted_iota(jnp.int32, (loaded, lanes), 1) == owner.astype(jnp.int32)).astype(
        jnp.float32
    )
    counts = jnp.dot(
        (second < first).astype(jnp.bfloat16), named.astype(jnp.bfloat16),
        preferred_element_type=jnp.float32,
    )
    slot = jnp.sum(named * counts, axis=1, keepdims=True)
    target = owner * capacity + slot
    target_row = jnp.sum(jnp.where(first == second, target, 0.0), axis=0, keepdims=True)
    placing = lax.broadcasted_iota(jnp.int32, (slots, loaded), 0) == target_row.astype(jnp.int32)
    present = jnp.sum(
        jnp.where(placing, valid_in[...].astype(jnp.float32), 0.0), axis=1, keepdims=True
    )
    placed = jnp.dot(
        placing.astype(jnp.bfloat16), frames_in[...], preferred_element_type=jnp.float32
    )
    outgoing[...] = (
        jnp.where(present > 0.5, placed, filler).astype(jnp.bfloat16).reshape(outgoing.shape)
    )

    pl.semaphore_wait(barrier, peers - 1 + groups - 1)

    def remote(src, dst, send, recv, **device):
        return pltpu.make_async_remote_copy(
            src_ref=src, dst_ref=dst, send_sem=send, recv_sem=recv,
            device_id=device, device_id_type=MESH,
        )

    def rows_copy(step):
        peer = lax.rem(me + step, peers)
        return remote(
            outgoing.at[peer], whole.at[column, me], rows_send.at[peer], rows_recv.at[me], dp=peer
        )

    def rows_arrival(step):
        peer = lax.rem(me + peers - step, peers)
        return remote(
            outgoing.at[peer], whole.at[column, peer], rows_send.at[peer], rows_recv.at[peer], dp=peer
        )

    for step in range(1, peers):
        rows_copy(step).start()
    whole[column, me] = outgoing[me]

    def part(shard, cut):
        return weights.at[cut, pl.ds(pl.multiple_of(shard * depth, depth), depth)]

    def weight_copy(where, source, cut, peer):
        shard = source * 2 + core
        return remote(
            part(shard, cut), part(shard, cut), where.at[source, cut], w_recv.at[shard, cut], dp=peer
        )

    def weight_arrival(shard, cut):
        return remote(
            part(shard, cut), part(shard, cut), w_side.at[0, cut], w_recv.at[shard, cut], dp=twin
        )

    def send_own(cut):
        if cut < cuts:
            pl.when(last)(lambda: weight_copy(w_up, chip, cut, above).start())
            pl.when(inner)(lambda: weight_copy(w_down, chip, cut, below).start())

    for cut in range(cuts):
        for load in loads[5 + 2 * cut:7 + 2 * cut]:
            load.wait()
        if cut == 0:
            send_own(cut)
        weight_copy(w_side, chip, cut, twin).start()

    def relay(cut, step, onward):
        @pl.when((chip >= step) & (last if onward else jnp.logical_not(last)))
        def _():
            source = chip - step
            weight_arrival(source * 2 + core, cut).wait_recv()
            if onward:
                weight_copy(w_up, source, cut, above).start()
            weight_copy(w_side, source, cut, twin).start()

        @pl.when((chip + step < chips) & (inner if onward else jnp.logical_not(inner)))
        def _():
            source = chip + step
            weight_arrival(source * 2 + core, cut).wait_recv()
            if onward:
                weight_copy(w_down, source, cut, below).start()
            weight_copy(w_side, source, cut, twin).start()

    def mp_copy(step, owned):
        peer = lax.rem(column + step, groups)
        return remote(
            whole.at[column, owned], whole.at[column, owned], mp_send.at[peer, owned],
            mp_recv.at[column, owned], mp=peer,
        )

    def mp_arrival(step, owned):
        peer = lax.rem(column + step, groups)
        return remote(
            whole.at[peer, owned], whole.at[peer, owned], mp_send.at[peer, owned],
            mp_recv.at[peer, owned], mp=peer,
        )

    for behind in range(peers):
        if behind:
            rows_arrival(behind).wait_recv()
        for step in range(1, groups):
            mp_copy(step, lax.rem(me + peers - behind, peers)).start()
    def relays(cut, steps):
        if cut < cuts:
            for step in steps:
                relay(cut, step, True)
                if step == 1:
                    send_own(cut + 1)

    relays(0, range(1, chips))
    if chips < 2:
        for cut in range(1, cuts):
            send_own(cut)
    relays(1, range(1, min(2, chips)))
    for behind in range(peers):
        for step in range(1, groups):
            mp_arrival(step, lax.rem(me + peers - behind, peers)).wait_recv()
    loads[3].wait()
    loads[4].wait()
    gain = gain_in[...].reshape(1, channels)

    def block(group):
        return whole[group].reshape(slots, width).astype(jnp.float32)

    live = block(0)[:, :1] < 0.5 * filler
    live_col = live.astype(jnp.float32)
    total = jnp.zeros((slots, 1), jnp.float32)
    for group in range(groups):
        total += jnp.sum(block(group), axis=1, keepdims=True)
    row_mean = jnp.where(live, total / channels, 0.0)
    square = jnp.zeros((slots, 1), jnp.float32)
    for group in range(groups):
        centred = jnp.where(live, block(group) - row_mean, 0.0)
        square += jnp.sum(centred * centred, axis=1, keepdims=True)
    factor = lax.rsqrt(square / channels + epsilon)
    for group in range(groups):
        at = slice(group * width, (group + 1) * width)
        centred = jnp.where(live, block(group) - row_mean, 0.0)
        wide = centred * factor * gain[:, at] * live_col
        normed[:, at] = wide.astype(jnp.bfloat16)
        normed_t[at, :] = wide.T.astype(jnp.bfloat16)

    def rows_of(shard):
        return pl.ds(pl.multiple_of(shard * depth, depth), depth)

    def t_copy(target):
        return remote(
            normed_t.at[rows_of(target * 2 + 1 - core)], sibling_t.at[target],
            t_send.at[target], t_recv.at[target], dp=twin,
        )

    for target in range(chips):
        t_copy(target).start()
    def delta_copy(cut):
        return remote(delta.at[cut], sibling_delta.at[cut], d_send.at[cut], d_recv.at[cut], dp=twin)

    def project(cut):
        for step in range(1, chips):
            relay(cut, step, False)
        for source in range(chips):
            weight_arrival(source * 2 + 1 - core, cut).wait_recv()
        act = jnp.dot(normed[...], weights[cut], preferred_element_type=jnp.float32)
        at = slice(cut * 128, (cut + 1) * 128)
        value_act = act[:, :128]
        gate_sig = jax.nn.sigmoid(act[:, 128:])
        upstream = upstream_in[:, at].astype(jnp.float32)
        delta[cut, :, :128] = (upstream * gate_sig * live_col).astype(jnp.bfloat16)
        delta[cut, :, 128:] = (
            upstream * value_act * gate_sig * (1.0 - gate_sig) * live_col
        ).astype(jnp.bfloat16)
        delta_copy(cut).start()
        gated_ref[:, at] = (value_act * gate_sig).astype(jnp.bfloat16)

    def term(group):
        rows = pl.ds(pl.multiple_of(group * width, width), width)
        result = jnp.zeros((slots, width), jnp.float32)
        for cut in range(cuts):
            result += lax.dot_general(
                delta[cut], weights[cut, rows, :], (((1,), (1,)), ((), ())),
                preferred_element_type=jnp.float32,
            )
        return result.astype(jnp.bfloat16)

    def x_copy(step):
        peer = lax.rem(column + step, groups)
        return remote(term_out.at[peer], term_in.at[column], x_send.at[peer], x_recv.at[column], mp=peer)

    def x_arrival(step):
        peer = lax.rem(column + step, groups)
        return remote(term_out.at[peer], term_in.at[peer], x_send.at[peer], x_recv.at[peer], mp=peer)

    def chip_sum(target, cut):
        return jnp.dot(
            normed_t[rows_of(target * 2 + core), :], delta[cut], preferred_element_type=jnp.float32
        ) + jnp.dot(sibling_t[target], sibling_delta[cut], preferred_element_type=jnp.float32)

    def hop(out, into, send, recv, target, cut, peer):
        return remote(
            out.at[cut, target], into.at[cut, target], send.at[cut, target], recv.at[cut, target],
            dp=peer,
        )

    def up(target, cut, peer):
        return hop(to_above, from_below, up_send, up_recv, target, cut, peer)

    def down(target, cut, peer):
        return hop(to_below, from_above, down_send, down_recv, target, cut, peer)

    def send_sum(copy, out, into, target, cut, onward, behind, ahead):
        own = chip_sum(target, cut)

        @pl.when(onward)
        def _():
            copy(target, cut, behind).wait_recv()
            out[cut, target] = (own + into[cut, target].astype(jnp.float32)).astype(jnp.bfloat16)

        @pl.when(jnp.logical_not(onward))
        def _():
            out[cut, target] = own.astype(jnp.bfloat16)

        copy(target, cut, ahead).start()

    def chain(cut):
        for step in range(chips - 1, 0, -1):
            relays(cut + 2, range(chips - step, chips - step + 1))
            @pl.when(chip + step < chips)
            def _():
                send_sum(up, to_above, from_below, chip + step, cut, inner, below, above)

            @pl.when(chip >= step)
            def _():
                send_sum(down, to_below, from_above, chip - step, cut, last, above, below)

    relays(1, range(2, chips))
    project(0)
    for target in range(chips):
        t_copy(target).wait_recv()
    for cut in range(cuts):
        delta_copy(cut).wait_recv()
        if cut == cuts - 1:
            for step in range(1, groups):
                peer = lax.rem(column + step, groups)
                term_out[peer] = term(peer)
                x_copy(step).start()
        chain(cut)
        if cut < cuts - 1:
            project(cut + 1)

    for cut in range(cuts):
        at = slice(cut * 128, (cut + 1) * 128)
        own = chip_sum(chip, cut)
        value_grad_ref[:, at] = own[:, :128]
        gate_grad_ref[:, at] = own[:, 128:]

    input_grad = term(column).astype(jnp.float32)
    for step in range(1, groups):
        x_arrival(step).wait_recv()
        input_grad += term_in[lax.rem(column + step, groups)].astype(jnp.float32)
    input_grad_ref[...] = input_grad.astype(jnp.bfloat16)

    def add(arrived, cut):
        at = slice(cut * 128, (cut + 1) * 128)
        value_grad_ref[:, at] += arrived[cut, chip, :, :128].astype(jnp.float32)
        gate_grad_ref[:, at] += arrived[cut, chip, :, 128:].astype(jnp.float32)

    for cut in range(cuts):
        @pl.when(inner)
        def _():
            up(chip, cut, below).wait_recv()
            add(from_below, cut)

        @pl.when(last)
        def _():
            down(chip, cut, above).wait_recv()
            add(from_above, cut)

    value_grad_ref[...] *= scale
    gate_grad_ref[...] *= scale

    for step in range(1, peers):
        rows_copy(step).wait_send()
    for step in range(1, groups):
        for owned in range(peers):
            mp_copy(step, owned).wait_send()
        x_copy(step).wait_send()
    for source in range(chips):
        t_copy(source).wait_send()
    for cut in range(cuts):
        delta_copy(cut).wait_send()
        for source in range(chips):
            weight_copy(w_side, source, cut, twin).wait_send()
            pl.when(last & (source <= chip))(lambda: weight_copy(w_up, source, cut, above).wait_send())
            pl.when(inner & (source >= chip))(lambda: weight_copy(w_down, source, cut, below).wait_send())
            pl.when(source > chip)(lambda: up(source, cut, above).wait_send())
            pl.when(source < chip)(lambda: down(source, cut, below).wait_send())


def write_out(*refs):
    count = len(refs) // 3
    for i, (source, result, held) in enumerate(
        zip(refs[:count], refs[count:2 * count], refs[2 * count:3 * count])
    ):
        pltpu.make_async_copy(source, held, refs[-1].at[0, i]).start()
    for i, (source, result, held) in enumerate(
        zip(refs[:count], refs[count:2 * count], refs[2 * count:3 * count])
    ):
        pltpu.make_async_copy(source, held, refs[-1].at[0, i]).wait()
        pltpu.make_async_copy(held, result, refs[-1].at[1, i]).start()
    for i, (result, held) in enumerate(zip(refs[count:2 * count], refs[2 * count:3 * count])):
        pltpu.make_async_copy(held, result, refs[-1].at[1, i]).wait()


def body(frames, frame_owner, frame_valid, norm_gain, value_weight, gate_weight, grad_owned):
    peers, groups = lax.axis_size("dp"), lax.axis_size("mp")
    capacity = grad_owned.shape[2]
    loaded, width = frames.shape
    depth = value_weight.shape[0]
    if peers % 2 or depth % 16 or capacity % 16 or loaded % 16 or width % 128 or groups * width != peers * depth:
        return plain_body(
            frames, frame_owner, frame_valid, norm_gain, value_weight, gate_weight, grad_owned
        )
    slots, chips, channels = peers * capacity, peers // 2, width * groups
    cuts = width // 128
    half, full = jnp.bfloat16, jnp.float32
    dma = pltpu.SemaphoreType.DMA
    hop = pltpu.VMEM((cuts, chips, depth, 256), half)
    deltas = pltpu.VMEM((cuts, slots, 256), half)
    vmem, hbm = pl.BlockSpec(memory_space=pltpu.VMEM), pl.BlockSpec(memory_space=pltpu.HBM)
    outs = (
        jax.ShapeDtypeStruct((slots, width), half),
        jax.ShapeDtypeStruct((depth, width), full),
        jax.ShapeDtypeStruct((depth, width), full),
        jax.ShapeDtypeStruct((slots, width), half),
    )
    results = pl.pallas_call(
        functools.partial(kernel, peers, groups, capacity, float(loaded * peers) ** (-0.5)),
        out_shape=outs,
        in_specs=[hbm] * 7,
        out_specs=(vmem,) * 4,
        scratch_shapes=[
            pltpu.VMEM((loaded, width), half),
            pltpu.VMEM((1, loaded), jnp.int32),
            pltpu.VMEM((1, loaded), jnp.int32),
            pltpu.VMEM((channels,), full),
            pltpu.VMEM((slots, width), half),
            pltpu.VMEM((peers, capacity, width), half),
            pltpu.VMEM((groups, peers, capacity, width), half),
            pltpu.VMEM((cuts, channels, 256), half),
            pltpu.VMEM((slots, channels), half),
            pltpu.VMEM((channels, slots), half),
            pltpu.VMEM((chips, depth, slots), half),
            deltas, deltas,
            hop, hop, hop, hop,
            pltpu.VMEM((groups, slots, width), half),
            pltpu.VMEM((groups, slots, width), half),
            dma((5 + 2 * cuts,)),
            dma((peers,)), dma((peers,)), dma((groups, peers)), dma((groups, peers)),
            dma((chips, cuts)), dma((chips, cuts)), dma((chips, cuts)), dma((peers, cuts)),
            dma((chips,)), dma((chips,)), dma((cuts,)), dma((cuts,)),
            dma((cuts, chips)), dma((cuts, chips)), dma((cuts, chips)), dma((cuts, chips)),
            dma((groups,)), dma((groups,)),
        ],
        compiler_params=pltpu.CompilerParams(
            collective_id=0, has_side_effects=True, vmem_limit_bytes=63 * 1024 * 1024
        ),
    )(
        frames, frame_owner.reshape(1, loaded), frame_valid.reshape(1, loaded), norm_gain,
        value_weight, gate_weight, grad_owned.reshape(slots, width),
    )
    gated, value_grad, gate_grad, input_grad = pl.pallas_call(
        write_out,
        out_shape=outs,
        in_specs=[hbm] * 4,
        out_specs=(hbm,) * 4,
        scratch_shapes=[pltpu.VMEM(out.shape, out.dtype) for out in outs] + [dma((2, 4))],
    )(*results)
    return (
        gated.reshape(1, peers, capacity, width), value_grad, gate_grad,
        input_grad.reshape(1, peers, capacity, width),
    )


def solution(mesh):
    placed = (
        P("dp", "mp"),
        P("dp", None),
        P("dp"),
        P(),
        P("dp", "mp"),
        P("dp", "mp"),
        P("dp", None, None, "mp"),
    )
    return jax.shard_map(
        body,
        mesh=mesh,
        in_specs=placed,
        out_specs=(
            P("dp", None, None, "mp"),
            P("dp", "mp"),
            P("dp", "mp"),
            P("dp", None, None, "mp"),
        ),
        check_vma=False,
    )
```
